512 devices in a mesh: row: 8 (over y, core), col: 32 (over z_lo, x), leaf: 2 (over z_hi).
Axes of the slice: x: 4, y: 4, z: 16 (z_hi: 2, z_lo: 8; z = z_hi * 8 + z_lo), core: 2. Of those that a mesh axis runs over, the one named last changes fastest.
Arguments:
- ancestor: bfloat16 [8192, 8192], P('row', ('col', 'leaf')), may hold values from -2 to 42, as said below
- factor: bfloat16 [8, 8192, 512], P(None, ('row', 'col', 'leaf')), may hold values from -0.03125 to 0.03125
- inv_diag: bfloat16 [8, 512, 512], replicated, may hold values from -0.4 to 2, as said below
- pattern: int32 [8, 32], replicated, may hold values 0 or 1
Outputs:
- sigma_panel: float32 [8, 8192, 512], P('row', ('col', 'leaf'))
- sigma_diag: float32 [8, 512, 512], P('row', ('col', 'leaf'))
The draws below stay inside these ranges and needn't reach their ends.
Inputs may be any that keep to these rules, and one draw needn't show every extreme that they name: ancestor is symmetric. Each inv_diag[j] is lower triangular with a positive diagonal.
All inputs are finite; a program needn't handle non-finite values.
Results may differ from the reference program's by a relative error of at most 0.0029.
Values may be sent and summed in bfloat16 or wider, within the bound.
A program may use at most 64 MiB of HBM per device.

```python
import math
import jax
import jax.numpy as jnp
from jax import lax

S = 8192
K = 512
BLOCK = 256
KIDS = 8
A = 32


def draw_ancestor(key, part):
    key = jax.random.fold_in(key, 11)
    spread_key, leading_key = jax.random.split(key)
    fluctuation = jnp.clip(jax.random.normal(spread_key, (S, S), jnp.float32), -4.0, 4.0) * 0.35
    leading = jnp.exp(jax.random.uniform(leading_key, (S,), jnp.float32, math.log(4.0), math.log(40.0)))
    symmetric = 0.5 * (fluctuation + fluctuation.T)
    diagonal_mask = jnp.arange(S)[:, None] == jnp.arange(S)[None, :]
    return jnp.where(diagonal_mask, leading[None, :] + symmetric, symmetric).astype(jnp.bfloat16)


def draw_inv_diag(key, part):
    key = jax.random.fold_in(key, 23)
    lower_key, leading_key = jax.random.split(key)
    lower_part = jnp.clip(jax.random.normal(lower_key, (KIDS, K, K), jnp.float32), -4.0, 4.0)
    leading = jnp.exp(jax.random.uniform(leading_key, (KIDS, K), jnp.float32, math.log(0.5), math.log(2.0)))
    row_ids = jnp.arange(K)[:, None]
    col_ids = jnp.arange(K)[None, :]
    strict = jnp.where(row_ids > col_ids, lower_part * (0.7 / math.sqrt(K)), 0.0)
    return jnp.where(row_ids == col_ids, leading[:, :, None], strict).astype(jnp.bfloat16)


def plant(array, own_key, least, high):
    longest = array.shape.index(max(array.shape))
    spots = []
    for shift in (0, 1):
        where = [jax.random.randint(jax.random.fold_in(own_key, axis), (), 0, length) for axis, length in enumerate(array.shape)]
        where[longest] = (where[longest] + shift) % array.shape[longest]
        spots.append(tuple(where))
    return array.at[spots[0]].set(least).at[spots[1]].set(high)


def level_of(rng, extent, shards, smallest, high):
    gain = 1.0
    for axis_at, blocks in shards:
        heights = jax.random.uniform(jax.random.fold_in(jax.random.fold_in(rng, 6), axis_at), (blocks,), jnp.float32, smallest / len(shards), high / len(shards))
        gain = gain * jnp.repeat(jnp.exp(heights), extent[axis_at] // blocks).reshape((-1,) + (1,) * (len(extent) - 1 - axis_at))
    return gain


def bell_draw(rng, dims, spread, reach, cuts=(), held_as=jnp.bfloat16):
    array = spread * jax.random.normal(rng, dims, jnp.float32)
    if cuts:
        array = array * level_of(rng, dims, cuts, -0.22, 0.18)
    return jnp.clip(array, -reach, reach).astype(held_as)


def setup_inputs(seed: int = 0) -> dict:
    seeds = jax.random.split(jax.random.key(seed), 5)
    return {
        "ancestor": draw_ancestor(jax.random.fold_in(seeds[4], 71), 0),
        "factor": bell_draw(seeds[1], (KIDS, S, K), (4 * S) ** -0.5, 0.03125, ((1, 512),)),
        "inv_diag": draw_inv_diag(jax.random.fold_in(seeds[4], 71), 0),
        "pattern": plant((jax.random.randint(seeds[3], (KIDS, A), 0, 4) < 3).astype(jnp.int32), jax.random.fold_in(seeds[3], 1), 0, 1),
    }


def block_keep(pattern):
    blocks = jnp.arange(S, dtype=jnp.int32) // BLOCK
    matches = blocks[:, None] == jnp.arange(pattern.shape[1], dtype=jnp.int32)[None, :]
    return jnp.sum(jnp.where(matches[None, :, :], pattern[:, None, :], 0), axis=2) > 0


def reference(ancestor, factor, inv_diag, pattern):
    kept = block_keep(pattern)
    masked = jnp.where(kept[:, :, None], factor, jnp.zeros_like(factor))

    def per_child(operands):
        child_rows, inverse, kept_rows = operands
        panel = jnp.dot(child_rows, inverse, preferred_element_type=jnp.float32).astype(jnp.bfloat16)
        product = jnp.dot(ancestor, panel, preferred_element_type=jnp.float32)
        out_panel = -jnp.where(kept_rows[:, None], product, jnp.zeros_like(product))
        rounded = product.astype(jnp.bfloat16)
        square = jnp.dot(inverse.T, inverse, preferred_element_type=jnp.float32)
        cross = jnp.dot(panel.T, rounded, preferred_element_type=jnp.float32)
        return out_panel, square + cross

    sigma_panel, sigma_diag = lax.map(per_child, (masked, inv_diag, kept))
    return sigma_panel, sigma_diag
```

```python
import functools

import jax
import jax.numpy as jnp
from jax import lax
from jax.experimental import pallas as pl
from jax.experimental.pallas import tpu as pltpu
from jax.sharding import PartitionSpec as P

MESH = pl.DeviceIdType.MESH
NX, NY, NZ, ZLO, ZHI = 4, 4, 16, 8, 2
F32, BF16 = jnp.float32, jnp.bfloat16


def device(x, y, z, h):
    return (2 * y + h, 4 * lax.rem(z, ZLO) + x, z // ZLO)


def contract_rows(a, b):
    return lax.dot_general(a, b, (((0,), (0,)), ((), ())), preferred_element_type=F32)


def kernel(
    a_ref, factor_ref, inv_ref, pattern_ref, out_ref, diag_ref,
    at, fbuf, pn, inv_own, inv_sq, square, o_send, o_recv, pd, cross, x_send, x_recv, z_send, z_recv,
    f_ss, f_rs, a_ss, a_rs, c_ss, c_rs, r_ss, r_rs, o_ss, o_rs, p_ss, p_rs, x_ss, x_rs, z_ss, z_rs, l_sem,
):
    row, col, z_hi = lax.axis_index("row"), lax.axis_index("col"), lax.axis_index("leaf")
    y, h = row // 2, lax.rem(row, 2)
    z_lo, x = col // 4, lax.rem(col, 4)
    z = z_hi * ZLO + z_lo
    band = col * 2 + z_hi

    def send(src, dst, ss, rs, to):
        return pltpu.make_async_remote_copy(
            src_ref=src, dst_ref=dst, send_sem=ss, recv_sem=rs, device_id=to, device_id_type=MESH
        )

    inv_copy = pltpu.make_async_copy(inv_ref.at[2 * x + h], inv_own, l_sem.at[0])
    sq_copy = pltpu.make_async_copy(inv_ref.at[row], inv_sq, l_sem.at[1])
    inv_copy.start()
    sq_copy.start()

    barrier = pltpu.get_barrier_semaphore()

    def greet(to):
        pl.semaphore_signal(barrier, inc=1, device_id=to, device_id_type=MESH)

    for k in range(1, 8):
        dx, dh = k // 2, k % 2
        greet(device(lax.rem(x + dx, NX), y, z, lax.rem(h + dh, 2)))
    for k in range(1, NZ):
        greet(device(x, y, lax.rem(z + k, NZ), h))
    for k in range(1, NY):
        greet(device(y, lax.rem(y + k, NY), z, h))

    @pl.when(x != y)
    def _():
        greet(device(y, y, z, h))

    pl.semaphore_wait(barrier, 7 + 15 + 3 + jnp.where(x != y, 1, 0))

    f_copies = []
    for k in range(1, 8):
        tx, th = lax.rem(x + k // 2, NX), lax.rem(h + k % 2, 2)
        f_copies.append(
            send(factor_ref.at[2 * tx + th], fbuf.at[h, x], f_ss.at[k], f_rs.at[k], device(tx, y, z, th))
        )
        f_copies[-1].start()
    fbuf[h, x] = factor_ref[2 * x + h]

    at[h, x] = a_ref[...].T
    a_copies = []
    for k in range(1, NX):
        a_copies.append(
            send(at.at[h, x], at.at[h, x], a_ss.at[k], a_rs.at[k], device(lax.rem(x + k, NX), y, z, h))
        )
        a_copies[-1].start()
    c_copies = []

    def to_sibling(k):
        sx = lax.rem(x + NX - k, NX)
        if k:
            a_copies[k - 1].wait_recv()
        c_copies.append(send(at.at[h, sx], at.at[h, sx], c_ss.at[k], c_rs.at[k], device(x, y, z, 1 - h)))
        c_copies[-1].start()

    to_sibling(0)

    inv_copy.wait()
    for c in f_copies:
        c.wait_recv()
    child = 2 * x + h
    pieces = []
    for hh in range(2):
        keep = pattern_ref[child, 4 * (2 * y + hh) + z_lo // 2]
        rows = fbuf[hh].reshape(64, 512)
        pieces.append((rows.astype(F32) * keep.astype(F32)).astype(BF16))
    masked = jnp.concatenate(pieces, axis=0)
    panel = jnp.dot(masked, inv_own[...], preferred_element_type=F32).astype(BF16)
    panel = panel.reshape(2, 4, 16, 512)
    for hh in range(2):
        for xx in range(4):
            pn[hh, z_lo, xx, z_hi] = panel[hh, xx]

    def shard(zz, hh):
        return pn.at[hh, lax.rem(zz, ZLO), :, zz // ZLO]

    ring = {}
    last = []
    for t in range(1, 9):
        for hh in range(2):
            for d in range(2):
                if t == 8 and d != hh:
                    last.append(ring[d, t - 1, hh])
                    continue
                if t > 1:
                    ring[d, t - 1, hh].wait_recv()
                if d == 0:
                    src, to = lax.rem(z + NZ - (t - 1), NZ), lax.rem(z + 1, NZ)
                else:
                    src, to = lax.rem(z + (t - 1), NZ), lax.rem(z + NZ - 1, NZ)
                ring[d, t, hh] = send(
                    shard(src, hh), shard(src, hh), r_ss.at[d, t - 1, hh], r_rs.at[d, t - 1, hh],
                    device(x, y, to, h),
                )
                ring[d, t, hh].start()
                if t == 8:
                    last.append(ring[d, t, hh])
        if t == 1:
            sq_copy.wait()
            lanes = pl.multiple_of((band * 8) // 128 * 128, 128)
            square[...] = contract_rows(inv_sq[:, pl.ds(lanes, 128)], inv_sq[...])
        if t == 6:
            to_sibling(1)
            to_sibling(3)
        if t == 7:
            to_sibling(2)
    for c in last:
        c.wait_recv()

    holds = y == z_lo // 2
    for xx in range(NX):
        here = jnp.logical_and(xx == x, x == y)

        @pl.when(jnp.logical_and(holds, jnp.logical_not(here)))
        def _():
            send(
                pn.at[lax.rem(z_lo, 2), 2 * xx + z_hi], pd, p_ss.at[xx], p_rs.at[0], device(xx, x, z, h)
            ).start()

        @pl.when(jnp.logical_and(holds, here))
        def _():
            pd[...] = pn[lax.rem(z_lo, 2), 2 * xx + z_hi]

    for c in c_copies:
        c.wait_recv()
    for xx in range(NX):
        part = jnp.dot(at[0, xx], pn[0].reshape(1024, 512), preferred_element_type=F32)
        part += jnp.dot(at[1, xx], pn[1].reshape(1024, 512), preferred_element_type=F32)
        o_send[xx] = part.astype(BF16)
        here = jnp.logical_and(xx == x, x == y)

        @pl.when(jnp.logical_not(here))
        def _():
            send(o_send.at[xx], o_recv.at[y], o_ss.at[xx], o_rs.at[y], device(xx, x, z, h)).start()

        @pl.when(here)
        def _():
            o_recv[y] = o_send[xx]

    for yy in range(NY):

        @pl.when(jnp.logical_not(jnp.logical_and(x == y, yy == y)))
        def _():
            send(o_send.at[0], o_recv.at[yy], o_ss.at[0], o_rs.at[yy], device(x, y, z, 1 - h)).wait_recv()

    total = o_recv[0].astype(F32) + o_recv[1].astype(F32) + o_recv[2].astype(F32) + o_recv[3].astype(F32)
    keep = pattern_ref[row, col]
    out_ref[0] = total * (-keep.astype(F32))

    @pl.when(jnp.logical_not(jnp.logical_and(x == y, holds)))
    def _():
        send(pn.at[0, 0], pd, p_ss.at[0], p_rs.at[0], device(x, y, z, 1 - h)).wait_recv()

    own_panel = pd[...].reshape(128, 512)
    cross[...] = contract_rows(own_panel, total.astype(BF16)).reshape(8, 4, 16, 512)
    x_send[...] = cross[...].astype(BF16)
    x_copies = []
    for k in range(1, NX):
        tx = lax.rem(x + k, NX)
        x_copies.append(send(x_send.at[:, tx], x_recv.at[k], x_ss.at[k], x_rs.at[k], device(tx, y, z, h)))
        x_copies[-1].start()
    mine = cross[:, x]
    for k in range(1, NX):
        x_copies[k - 1].wait_recv()
        mine += x_recv[k].astype(F32)
    mine = mine.reshape(8, 2, 8, 512)
    for hi in range(2):
        for lo in range(8):
            piece = mine[lo, hi]
            z_send[hi * 8 + lo] = jnp.concatenate([piece[:, :256], piece[:, 256:]], axis=0).astype(BF16)
    z_copies = []
    for k in range(1, NZ):
        tz = lax.rem(z + k, NZ)
        z_copies.append(send(z_send.at[tz], z_recv.at[k], z_ss.at[k], z_rs.at[k], device(x, y, tz, h)))
        z_copies[-1].start()
    acc = z_send[z].astype(F32)
    for k in range(1, NZ):
        z_copies[k - 1].wait_recv()
        acc += z_recv[k].astype(F32)
    own = square[pl.ds(pl.multiple_of(lax.rem(band * 8, 128), 8), 8), :]
    diag_ref[0, :, :256] = acc[:8] + own[:, :256]
    diag_ref[0, :, 256:] = acc[8:] + own[:, 256:]

    for c in f_copies + a_copies + c_copies + list(ring.values()) + x_copies + z_copies:
        c.wait_send()
    for xx in range(NX):
        here = jnp.logical_and(xx == x, x == y)

        @pl.when(jnp.logical_not(here))
        def _():
            send(o_send.at[xx], o_recv.at[y], o_ss.at[xx], o_rs.at[y], device(xx, x, z, h)).wait_send()

        @pl.when(jnp.logical_and(holds, jnp.logical_not(here)))
        def _():
            send(
                pn.at[lax.rem(z_lo, 2), 2 * xx + z_hi], pd, p_ss.at[xx], p_rs.at[0], device(xx, x, z, h)
            ).wait_send()


def body(ancestor, factor, inv_diag, pattern):
    vmem, dma = pltpu.VMEM, pltpu.SemaphoreType.DMA
    return pl.pallas_call(
        kernel,
        out_shape=(
            jax.ShapeDtypeStruct((1, 128, 512), F32),
            jax.ShapeDtypeStruct((1, 8, 512), F32),
        ),
        in_specs=[
            pl.BlockSpec(memory_space=pltpu.VMEM),
            pl.BlockSpec(memory_space=pltpu.VMEM),
            pl.BlockSpec(memory_space=pl.ANY),
            pl.BlockSpec(memory_space=pltpu.SMEM),
        ],
        out_specs=(pl.BlockSpec(memory_space=pltpu.VMEM), pl.BlockSpec(memory_space=pltpu.VMEM)),
        scratch_shapes=[
            vmem((2, 4, 128, 1024), BF16),
            vmem((2, 4, 16, 512), BF16),
            vmem((2, 8, 4, 2, 16, 512), BF16),
            vmem((512, 512), BF16),
            vmem((512, 512), BF16),
            vmem((128, 512), F32),
            vmem((4, 128, 512), BF16),
            vmem((4, 128, 512), BF16),
            vmem((4, 2, 16, 512), BF16),
            vmem((8, 4, 16, 512), F32),
            vmem((8, 4, 16, 512), BF16),
            vmem((4, 8, 16, 512), BF16),
            vmem((16, 16, 256), BF16),
            vmem((16, 16, 256), BF16),
            dma((8,)), dma((8,)),
            dma((4,)), dma((4,)),
            dma((4,)), dma((4,)),
            dma((2, 8, 2)), dma((2, 8, 2)),
            dma((4,)), dma((4,)),
            dma((4,)), dma((1,)),
            dma((4,)), dma((4,)),
            dma((16,)), dma((16,)),
            dma((2,)),
        ],
        compiler_params=pltpu.CompilerParams(
            collective_id=0, has_side_effects=True, vmem_limit_bytes=48 * 1024 * 1024
        ),
        name="takahashi",
    )(ancestor, factor, inv_diag, pattern)


def solution(mesh):
    return jax.shard_map(
        body,
        mesh=mesh,
        in_specs=(P("row", ("col", "leaf")), P(None, ("row", "col", "leaf"), None), P(), P()),
        out_specs=(P("row", ("col", "leaf"), None), P("row", ("col", "leaf"), None)),
        check_vma=False,
    )
```

```python
import functools

import jax
import jax.numpy as jnp
from jax import lax
from jax.experimental import pallas as pl
from jax.experimental.pallas import tpu as pltpu
from jax.sharding import PartitionSpec as P

MESH = pl.DeviceIdType.MESH
NX, NY, NZ, ZLO = 4, 4, 16, 8
F32, BF16 = jnp.float32, jnp.bfloat16


def device(x, y, z, h):
    return (2 * y + h, 4 * lax.rem(z, ZLO) + x, z // ZLO)


def contract_rows(a, b):
    return lax.dot_general(a, b, (((0,), (0,)), ((), ())), preferred_element_type=F32)


def both(*conditions):
    return functools.reduce(jnp.logical_and, conditions)


def kernel(
    a_hbm, factor_hbm, inv_hbm, pattern_hbm, out_ref, diag_ref,
    a_ref, factor_ref, pattern_ref, at, fbuf, pn, pc, inv_own, inv_sq, square, part, y_send, y_recv,
    o_send, o_recv, z_send, z_recv,
    f_ss, f_rs, a_ss, a_rs, c_ss, c_rs, r_ss, r_rs, p_ss, p_rs, y_ss, y_rs, o_ss, o_rs, z_ss, z_rs, l_sem,
):
    row, col, z_hi = lax.axis_index("row"), lax.axis_index("col"), lax.axis_index("leaf")
    y, h = row // 2, lax.rem(row, 2)
    z_lo, x = col // 4, lax.rem(col, 4)
    z = z_hi * ZLO + z_lo
    band = col * 2 + z_hi
    child = 2 * x + h

    def send(src, dst, ss, rs, to):
        return pltpu.make_async_remote_copy(
            src_ref=src, dst_ref=dst, send_sem=ss, recv_sem=rs, device_id=to, device_id_type=MESH
        )

    loads = [
        pltpu.make_async_copy(src, dst, l_sem.at[i])
        for i, (src, dst) in enumerate((
            (factor_hbm, factor_ref), (a_hbm, a_ref), (pattern_hbm, pattern_ref),
            (inv_hbm.at[child], inv_own), (inv_hbm.at[row], inv_sq),
        ))
    ]
    for c in loads:
        c.start()

    barrier = pltpu.get_barrier_semaphore()

    def greet(to):
        pl.semaphore_signal(barrier, inc=1, device_id=to, device_id_type=MESH)

    for k in range(1, 8):
        greet(device(lax.rem(x + k // 2, NX), y, z, lax.rem(h + k % 2, 2)))
    for k in (1, NZ - 1):
        greet(device(x, y, lax.rem(z + k, NZ), h))
    for k in range(1, NY):
        greet(device(x, lax.rem(y + k, NY), z, h))
    loads[0].wait()
    pl.semaphore_wait(barrier, 12)

    f_copies = []
    for k in range(1, 8):
        tx, th = lax.rem(x + k // 2, NX), lax.rem(h + k % 2, 2)
        f_copies.append(
            send(factor_ref.at[2 * tx + th], fbuf.at[h, x], f_ss.at[k], f_rs.at[k], device(tx, y, z, th))
        )
        f_copies[-1].start()
    fbuf[h, x] = factor_ref[child]

    loads[1].wait()
    at[h, x] = a_ref[...].T
    a_copies = []
    for k in range(1, NX):
        a_copies.append(
            send(at.at[h, x], at.at[h, x], a_ss.at[k], a_rs.at[k], device(lax.rem(x + k, NX), y, z, h))
        )
        a_copies[-1].start()
    c_copies = []

    def to_sibling(k):
        sx = lax.rem(x + NX - k, NX)
        if k:
            a_copies[k - 1].wait_recv()
        c_copies.append(send(at.at[h, sx], at.at[h, sx], c_ss.at[k], c_rs.at[k], device(x, y, z, 1 - h)))
        c_copies[-1].start()

    to_sibling(0)

    for c in loads[2:4]:
        c.wait()
    for c in f_copies:
        c.wait_recv()
    pieces = []
    for hh in range(2):
        keep = pattern_ref[child, 4 * (2 * y + hh) + z_lo // 2]
        pieces.append((fbuf[hh].reshape(64, 512).astype(F32) * keep.astype(F32)).astype(BF16))
    masked = jnp.concatenate(pieces, axis=0)
    panel = jnp.dot(masked, inv_own[...], preferred_element_type=F32).astype(BF16).reshape(2, 4, 16, 512)
    for hh in range(2):
        for xx in range(4):
            pn[hh, z_lo, xx, z_hi] = panel[hh, xx]

    holds = y == z_lo // 2

    def share(zz, hh):
        @pl.when(both(holds, lax.rem(z_lo, 2) == hh, lax.rem(zz, 2) == z_hi))
        def _():
            zl, zh = lax.rem(zz, ZLO), zz // ZLO
            for k in (1, 3, 2):
                send(
                    pn.at[hh, zl, :, zh], pc.at[zl // 2, :, zh], p_ss.at[zl // 2, zh, k], p_rs.at[zl // 2, zh],
                    device(x, lax.rem(y + k, NY), z, h),
                ).start()
            pc[zl // 2, :, zh] = pn[hh, zl, :, zh]

    def shard(zz, s):
        return pn.at[s // 2, lax.rem(zz, ZLO), pl.ds(s % 2 * 2, 2), zz // ZLO]

    ring = {}
    for t in range(1, 9):
        for s in range(4):
            for d in range(2):
                src = lax.rem(z + (NZ - (t - 1) if d == 0 else t - 1), NZ)
                to = lax.rem(z + (1 if d == 0 else NZ - 1), NZ)
                if t > 1:
                    ring[d, t - 1, s].wait_recv()
                if t < 8 or d == s // 2:
                    ring[d, t, s] = send(
                        shard(src, s), shard(src, s), r_ss.at[d, t - 1, s], r_rs.at[d, t - 1, s],
                        device(x, y, to, h),
                    )
                    ring[d, t, s].start()
                if s % 2 == 1 and (t > 1 or d == 0):
                    share(src, s // 2)
        if t == 1:
            loads[4].wait()
            lanes = pl.multiple_of((band * 8) // 128 * 128, 128)
            square[...] = contract_rows(inv_sq[:, pl.ds(lanes, 128)], inv_sq[...])
        if t == 6:
            to_sibling(1)
            to_sibling(3)
        if t == 7:
            to_sibling(2)
    for s in range(4):
        ring[s // 2, 8, s].wait_recv()
        if s % 2 == 1:
            share(lax.rem(z + 8, NZ), s // 2)

    for c in c_copies:
        c.wait_recv()
    for xx in range(NX):
        block = jnp.dot(at[0, xx], pn[0].reshape(1024, 512), preferred_element_type=F32)
        block += jnp.dot(at[1, xx], pn[1].reshape(1024, 512), preferred_element_type=F32)
        for yy in range(NY):
            columns = block[:, yy * 128 : yy * 128 + 128]
            part[yy, xx] = columns
            y_send[yy, xx] = columns.astype(BF16)
    y_copies = []
    for k in range(1, NY):
        ty = lax.rem(y + k, NY)
        y_copies.append(send(y_send.at[ty], y_recv.at[k], y_ss.at[k], y_rs.at[k], device(x, ty, z, h)))
        y_copies[-1].start()
    total = part[y]
    for k in range(1, NY):
        y_copies[k - 1].wait_recv()
        total += y_recv[k].astype(F32)

    o_send[...] = total
    for xx in range(NX):
        here = both(xx == x, x == y)

        @pl.when(jnp.logical_not(here))
        def _():
            send(o_send.at[xx], o_recv.at[y], o_ss.at[xx], o_rs.at[y], device(xx, x, z, h)).start()

        @pl.when(here)
        def _():
            o_recv[y] = o_send[xx]

    @pl.when(jnp.logical_not(holds))
    def _():
        for i in range(4):
            for zh in range(2):
                send(
                    pn.at[0, 0, :, 0], pc.at[i, :, zh], p_ss.at[i, zh, 0], p_rs.at[i, zh], device(x, y, z, 1 - h)
                ).wait_recv()

    cross = contract_rows(total.astype(BF16).reshape(512, 128), pc[...].reshape(512, 512)).reshape(16, 8, 512)
    for i in range(16):
        z_send[i] = jnp.concatenate([cross[i][:, :256], cross[i][:, 256:]], axis=0).astype(BF16)

    def piece(i):
        tx, tz = lax.rem(i // 2, 4), lax.rem(i, 2) * ZLO + 2 * y + i // 8
        return device(tx, x, tz, h), both(tx == x, x == y, tz == z)

    for n in range(16):
        i = lax.rem(z + n, 16)
        to, here = piece(i)

        @pl.when(jnp.logical_not(here))
        def _():
            send(z_send.at[i], z_recv.at[z], z_ss.at[i], z_rs.at[z], to).start()

        @pl.when(here)
        def _():
            z_recv[z] = z_send[i]

    keep = -pattern_ref[row, col].astype(F32)
    for yy in range(NY):

        @pl.when(jnp.logical_not(both(x == y, yy == y)))
        def _():
            send(o_send.at[0], o_recv.at[yy], o_ss.at[0], o_rs.at[yy], device(x, y, z, 1 - h)).wait_recv()

        out_ref[0, :, yy * 128 : yy * 128 + 128] = o_recv[yy] * keep
    for zz in range(NZ):

        @pl.when(jnp.logical_not(both(x == y, holds, zz == z)))
        def _():
            send(z_send.at[0], z_recv.at[zz], z_ss.at[0], z_rs.at[zz], device(x, y, z, 1 - h)).wait_recv()

    acc = z_recv[0].astype(F32)
    for zz in range(1, NZ):
        acc += z_recv[zz].astype(F32)
    own = square[pl.ds(pl.multiple_of(lax.rem(band * 8, 128), 8), 8), :]
    diag_ref[0, :, :256] = acc[:8] + own[:, :256]
    diag_ref[0, :, 256:] = acc[8:] + own[:, 256:]

    for c in f_copies + a_copies + c_copies + list(ring.values()) + y_copies:
        c.wait_send()

    @pl.when(holds)
    def _():
        for i in range(4):
            for zh in range(2):
                for k in (1, 2, 3):
                    send(
                        pn.at[0, 0, :, 0], pc.at[i, :, zh], p_ss.at[i, zh, k], p_rs.at[i, zh],
                        device(x, lax.rem(y + k, NY), z, h),
                    ).wait_send()

    for xx in range(NX):

        @pl.when(jnp.logical_not(both(xx == x, x == y)))
        def _():
            send(o_send.at[xx], o_recv.at[y], o_ss.at[xx], o_rs.at[y], device(xx, x, z, h)).wait_send()

    for i in range(16):
        to, here = piece(i)

        @pl.when(jnp.logical_not(here))
        def _():
            send(z_send.at[i], z_recv.at[z], z_ss.at[i], z_rs.at[z], to).wait_send()


def body(ancestor, factor, inv_diag, pattern):
    vmem, dma = pltpu.VMEM, pltpu.SemaphoreType.DMA
    return pl.pallas_call(
        kernel,
        out_shape=(
            jax.ShapeDtypeStruct((1, 128, 512), F32),
            jax.ShapeDtypeStruct((1, 8, 512), F32),
        ),
        in_specs=[pl.BlockSpec(memory_space=pl.ANY)] * 4,
        out_specs=(pl.BlockSpec(memory_space=pltpu.VMEM), pl.BlockSpec(memory_space=pltpu.VMEM)),
        scratch_shapes=[
            vmem((1024, 128), BF16),
            vmem((8, 16, 512), BF16),
            pltpu.SMEM((8, 32), jnp.int32),
            vmem((2, 4, 128, 1024), BF16),
            vmem((2, 4, 16, 512), BF16),
            vmem((2, 8, 4, 2, 16, 512), BF16),
            vmem((4, 4, 2, 16, 512), BF16),
            vmem((512, 512), BF16),
            vmem((512, 512), BF16),
            vmem((128, 512), F32),
            vmem((4, 4, 128, 128), F32),
            vmem((4, 4, 128, 128), BF16),
            vmem((4, 4, 128, 128), BF16),
            vmem((4, 128, 128), F32),
            vmem((4, 128, 128), F32),
            vmem((16, 16, 256), BF16),
            vmem((16, 16, 256), BF16),
            dma((8,)), dma((8,)),
            dma((4,)), dma((4,)),
            dma((4,)), dma((4,)),
            dma((2, 8, 4)), dma((2, 8, 4)),
            dma((4, 2, 4)), dma((4, 2)),
            dma((4,)), dma((4,)),
            dma((4,)), dma((4,)),
            dma((16,)), dma((16,)),
            dma((5,)),
        ],
        compiler_params=pltpu.CompilerParams(
            collective_id=0, has_side_effects=True, vmem_limit_bytes=60 * 1024 * 1024
        ),
        name="takahashi",
    )(ancestor, factor, inv_diag, pattern)


def solution(mesh):
    return jax.shard_map(
        body,
        mesh=mesh,
        in_specs=(P("row", ("col", "leaf")), P(None, ("row", "col", "leaf"), None), P(), P()),
        out_specs=(P("row", ("col", "leaf"), None), P("row", ("col", "leaf"), None)),
        check_vma=False,
    )
```

```python
import functools

import jax
import jax.numpy as jnp
from jax import lax
from jax.experimental import pallas as pl
from jax.experimental.pallas import tpu as pltpu
from jax.sharding import PartitionSpec as P

MESH = pl.DeviceIdType.MESH
NX, NY, NZ, ZLO = 4, 4, 16, 8
F32, BF16 = jnp.float32, jnp.bfloat16


def device(x, y, z, h):
    return (2 * y + h, 4 * lax.rem(z, ZLO) + x, z // ZLO)


def contract_rows(a, b):
    return lax.dot_general(a, b, (((0,), (0,)), ((), ())), preferred_element_type=F32)


def both(*conditions):
    return functools.reduce(jnp.logical_and, conditions)


def kernel(
    a_hbm, factor_hbm, inv_hbm, pattern_hbm, out_ref, diag_ref,
    a_ref, factor_ref, pattern_ref, at, fbuf, pn, pc, inv_own, inv_sq, square, part, y_send, y_recv,
    o_send, o_recv, z_send, z_recv,
    f_ss, f_rs, a_ss, a_rs, c_ss, c_rs, r_ss, r_rs, p_ss, p_rs, y_ss, y_rs, o_ss, o_rs, z_ss, z_rs, l_sem,
):
    row, col, z_hi = lax.axis_index("row"), lax.axis_index("col"), lax.axis_index("leaf")
    y, h = row // 2, lax.rem(row, 2)
    z_lo, x = col // 4, lax.rem(col, 4)
    z = z_hi * ZLO + z_lo
    band = col * 2 + z_hi
    child = 2 * x + h

    def send(src, dst, ss, rs, to):
        return pltpu.make_async_remote_copy(
            src_ref=src, dst_ref=dst, send_sem=ss, recv_sem=rs, device_id=to, device_id_type=MESH
        )

    loads = [
        pltpu.make_async_copy(src, dst, l_sem.at[i])
        for i, (src, dst) in enumerate((
            (factor_hbm, factor_ref), (a_hbm, a_ref), (pattern_hbm, pattern_ref),
            (inv_hbm.at[child], inv_own), (inv_hbm.at[row], inv_sq),
        ))
    ]
    for c in loads:
        c.start()

    barrier = pltpu.get_barrier_semaphore()

    def greet(to):
        pl.semaphore_signal(barrier, inc=1, device_id=to, device_id_type=MESH)

    for k in range(1, 8):
        greet(device(lax.rem(x + k // 2, NX), y, z, lax.rem(h + k % 2, 2)))
    for k in (1, NZ - 1):
        greet(device(x, y, lax.rem(z + k, NZ), h))
    for k in range(1, NY):
        greet(device(x, lax.rem(y + k, NY), z, h))
    loads[0].wait()
    pl.semaphore_wait(barrier, 12)

    f_copies = []
    for k in range(1, 8):
        tx, th = lax.rem(x + k // 2, NX), lax.rem(h + k % 2, 2)
        f_copies.append(
            send(factor_ref.at[2 * tx + th], fbuf.at[h, x], f_ss.at[k], f_rs.at[k], device(tx, y, z, th))
        )
        f_copies[-1].start()
    fbuf[h, x] = factor_ref[child]

    a_copies = []
    c_copies = []

    def to_sibling(k):
        sx = lax.rem(x + NX - k, NX)
        if k:
            a_copies[k - 1].wait_recv()
        c_copies.append(send(at.at[h, sx], at.at[h, sx], c_ss.at[k], c_rs.at[k], device(x, y, z, 1 - h)))
        c_copies[-1].start()

    for c in loads[2:4]:
        c.wait()
    for c in f_copies:
        c.wait_recv()
    pieces = []
    for hh in range(2):
        keep = pattern_ref[child, 4 * (2 * y + hh) + z_lo // 2]
        pieces.append((fbuf[hh].reshape(64, 512).astype(F32) * keep.astype(F32)).astype(BF16))
    masked = jnp.concatenate(pieces, axis=0)
    panel = jnp.dot(masked, inv_own[...], preferred_element_type=F32).astype(BF16).reshape(2, 4, 16, 512)
    for hh in range(2):
        for xx in range(4):
            pn[hh, z_lo, xx, z_hi] = panel[hh, xx]

    holds = y == z_lo // 2

    def share(zz, hh):
        @pl.when(both(holds, lax.rem(z_lo, 2) == hh, lax.rem(zz, 2) == z_hi))
        def _():
            zl, zh = lax.rem(zz, ZLO), zz // ZLO
            for k in (1, 3, 2):
                send(
                    pn.at[hh, zl, :, zh], pc.at[zl // 2, :, zh], p_ss.at[zl // 2, zh, k], p_rs.at[zl // 2, zh],
                    device(x, lax.rem(y + k, NY), z, h),
                ).start()
            pc[zl // 2, :, zh] = pn[hh, zl, :, zh]

    def shard(zz, s):
        return pn.at[s // 2, lax.rem(zz, ZLO), pl.ds(s % 2 * 2, 2), zz // ZLO]

    ring = {}
    for t in range(1, 9):
        for s in range(4):
            for d in range(2):
                src = lax.rem(z + (NZ - (t - 1) if d == 0 else t - 1), NZ)
                to = lax.rem(z + (1 if d == 0 else NZ - 1), NZ)
                if t > 1:
                    ring[d, t - 1, s].wait_recv()
                if t < 8 or d == s // 2:
                    ring[d, t, s] = send(
                        shard(src, s), shard(src, s), r_ss.at[d, t - 1, s], r_rs.at[d, t - 1, s],
                        device(x, y, to, h),
                    )
                    ring[d, t, s].start()
                if s % 2 == 1 and (t > 1 or d == 0):
                    share(src, s // 2)
        if t == 1:
            loads[1].wait()
            at[h, x] = a_ref[...].T
            for k in range(1, NX):
                a_copies.append(
                    send(at.at[h, x], at.at[h, x], a_ss.at[k], a_rs.at[k], device(lax.rem(x + k, NX), y, z, h))
                )
                a_copies[-1].start()
            to_sibling(0)
            loads[4].wait()
            lanes = pl.multiple_of((band * 8) // 128 * 128, 128)
            square[...] = contract_rows(inv_sq[:, pl.ds(lanes, 128)], inv_sq[...])
        if t == 6:
            to_sibling(1)
            to_sibling(3)
        if t == 7:
            to_sibling(2)
    for s in range(4):
        ring[s // 2, 8, s].wait_recv()
        if s % 2 == 1:
            share(lax.rem(z + 8, NZ), s // 2)

    for c in c_copies:
        c.wait_recv()
    for xx in range(NX):
        block = jnp.dot(at[0, xx], pn[0].reshape(1024, 512), preferred_element_type=F32)
        block += jnp.dot(at[1, xx], pn[1].reshape(1024, 512), preferred_element_type=F32)
        for yy in range(NY):
            columns = block[:, yy * 128 : yy * 128 + 128]
            part[yy, xx] = columns
            y_send[yy, xx] = columns.astype(BF16)
    y_copies = []
    for k in range(1, NY):
        ty = lax.rem(y + k, NY)
        y_copies.append(send(y_send.at[ty], y_recv.at[k], y_ss.at[k], y_rs.at[k], device(x, ty, z, h)))
        y_copies[-1].start()
    total = part[y]
    for k in range(1, NY):
        y_copies[k - 1].wait_recv()
        total += y_recv[k].astype(F32)

    o_send[...] = total
    for xx in range(NX):
        here = both(xx == x, x == y)

        @pl.when(jnp.logical_not(here))
        def _():
            send(o_send.at[xx], o_recv.at[y], o_ss.at[xx], o_rs.at[y], device(xx, x, z, h)).start()

        @pl.when(here)
        def _():
            o_recv[y] = o_send[xx]

    @pl.when(jnp.logical_not(holds))
    def _():
        for i in range(4):
            for zh in range(2):
                send(
                    pn.at[0, 0, :, 0], pc.at[i, :, zh], p_ss.at[i, zh, 0], p_rs.at[i, zh], device(x, y, z, 1 - h)
                ).wait_recv()

    cross = contract_rows(total.astype(BF16).reshape(512, 128), pc[...].reshape(512, 512)).reshape(16, 8, 512)
    for i in range(16):
        z_send[i] = jnp.concatenate([cross[i][:, :256], cross[i][:, 256:]], axis=0).astype(BF16)

    def piece(i):
        tx, tz = lax.rem(i // 2, 4), lax.rem(i, 2) * ZLO + 2 * y + i // 8
        return device(tx, x, tz, h), both(tx == x, x == y, tz == z)

    for n in range(16):
        i = lax.rem(z + n, 16)
        to, here = piece(i)

        @pl.when(jnp.logical_not(here))
        def _():
            send(z_send.at[i], z_recv.at[z], z_ss.at[i], z_rs.at[z], to).start()

        @pl.when(here)
        def _():
            z_recv[z] = z_send[i]

    keep = -pattern_ref[row, col].astype(F32)
    for yy in range(NY):

        @pl.when(jnp.logical_not(both(x == y, yy == y)))
        def _():
            send(o_send.at[0], o_recv.at[yy], o_ss.at[0], o_rs.at[yy], device(x, y, z, 1 - h)).wait_recv()

        out_ref[0, :, yy * 128 : yy * 128 + 128] = o_recv[yy] * keep
    for zz in range(NZ):

        @pl.when(jnp.logical_not(both(x == y, holds, zz == z)))
        def _():
            send(z_send.at[0], z_recv.at[zz], z_ss.at[0], z_rs.at[zz], device(x, y, z, 1 - h)).wait_recv()

    acc = z_recv[0].astype(F32)
    for zz in range(1, NZ):
        acc += z_recv[zz].astype(F32)
    own = square[pl.ds(pl.multiple_of(lax.rem(band * 8, 128), 8), 8), :]
    diag_ref[0, :, :256] = acc[:8] + own[:, :256]
    diag_ref[0, :, 256:] = acc[8:] + own[:, 256:]

    for c in f_copies + a_copies + c_copies + list(ring.values()) + y_copies:
        c.wait_send()

    @pl.when(holds)
    def _():
        for i in range(4):
            for zh in range(2):
                for k in (1, 2, 3):
                    send(
                        pn.at[0, 0, :, 0], pc.at[i, :, zh], p_ss.at[i, zh, k], p_rs.at[i, zh],
                        device(x, lax.rem(y + k, NY), z, h),
                    ).wait_send()

    for xx in range(NX):

        @pl.when(jnp.logical_not(both(xx == x, x == y)))
        def _():
            send(o_send.at[xx], o_recv.at[y], o_ss.at[xx], o_rs.at[y], device(xx, x, z, h)).wait_send()

    for i in range(16):
        to, here = piece(i)

        @pl.when(jnp.logical_not(here))
        def _():
            send(z_send.at[i], z_recv.at[z], z_ss.at[i], z_rs.at[z], to).wait_send()


def body(ancestor, factor, inv_diag, pattern):
    vmem, dma = pltpu.VMEM, pltpu.SemaphoreType.DMA
    return pl.pallas_call(
        kernel,
        out_shape=(
            jax.ShapeDtypeStruct((1, 128, 512), F32),
            jax.ShapeDtypeStruct((1, 8, 512), F32),
        ),
        in_specs=[pl.BlockSpec(memory_space=pl.ANY)] * 4,
        out_specs=(pl.BlockSpec(memory_space=pltpu.VMEM), pl.BlockSpec(memory_space=pltpu.VMEM)),
        scratch_shapes=[
            vmem((1024, 128), BF16),
            vmem((8, 16, 512), BF16),
            pltpu.SMEM((8, 32), jnp.int32),
            vmem((2, 4, 128, 1024), BF16),
            vmem((2, 4, 16, 512), BF16),
            vmem((2, 8, 4, 2, 16, 512), BF16),
            vmem((4, 4, 2, 16, 512), BF16),
            vmem((512, 512), BF16),
            vmem((512, 512), BF16),
            vmem((128, 512), F32),
            vmem((4, 4, 128, 128), F32),
            vmem((4, 4, 128, 128), BF16),
            vmem((4, 4, 128, 128), BF16),
            vmem((4, 128, 128), F32),
            vmem((4, 128, 128), F32),
            vmem((16, 16, 256), BF16),
            vmem((16, 16, 256), BF16),
            dma((8,)), dma((8,)),
            dma((4,)), dma((4,)),
            dma((4,)), dma((4,)),
            dma((2, 8, 4)), dma((2, 8, 4)),
            dma((4, 2, 4)), dma((4, 2)),
            dma((4,)), dma((4,)),
            dma((4,)), dma((4,)),
            dma((16,)), dma((16,)),
            dma((5,)),
        ],
        compiler_params=pltpu.CompilerParams(
            collective_id=0, has_side_effects=True, vmem_limit_bytes=60 * 1024 * 1024
        ),
        name="takahashi",
    )(ancestor, factor, inv_diag, pattern)


def solution(mesh):
    return jax.shard_map(
        body,
        mesh=mesh,
        in_specs=(P("row", ("col", "leaf")), P(None, ("row", "col", "leaf"), None), P(), P()),
        out_specs=(P("row", ("col", "leaf"), None), P("row", ("col", "leaf"), None)),
        check_vma=False,
    )
```

```python
import functools

import jax
import jax.numpy as jnp
from jax import lax
from jax.experimental import pallas as pl
from jax.experimental.pallas import tpu as pltpu
from jax.sharding import PartitionSpec as P

MESH = pl.DeviceIdType.MESH
NX, NY, NZ, ZLO = 4, 4, 16, 8
F32, BF16 = jnp.float32, jnp.bfloat16


def device(x, y, z, h):
    return (2 * y + h, 4 * lax.rem(z, ZLO) + x, z // ZLO)


def contract_rows(a, b):
    return lax.dot_general(a, b, (((0,), (0,)), ((), ())), preferred_element_type=F32)


def both(*conditions):
    return functools.reduce(jnp.logical_and, conditions)


def kernel(
    a_hbm, factor_hbm, inv_hbm, pattern_hbm, out_hbm, diag_hbm,
    out_ref, diag_ref,    a_ref, factor_ref, pattern_ref, at, fbuf, pn, pc, inv_own, inv_sq, square, part, y_send, y_recv,
    o_send, o_recv, z_send, z_recv,
    f_ss, f_rs, a_ss, a_rs, c_ss, c_rs, r_ss, r_rs, p_ss, p_rs, y_ss, y_rs, o_ss, o_rs, z_ss, z_rs, l_sem,
):
    row, col, z_hi = lax.axis_index("row"), lax.axis_index("col"), lax.axis_index("leaf")
    y, h = row // 2, lax.rem(row, 2)
    z_lo, x = col // 4, lax.rem(col, 4)
    z = z_hi * ZLO + z_lo
    band = col * 2 + z_hi
    child = 2 * x + h

    def send(src, dst, ss, rs, to):
        return pltpu.make_async_remote_copy(
            src_ref=src, dst_ref=dst, send_sem=ss, recv_sem=rs, device_id=to, device_id_type=MESH
        )

    def all_in(like, sem):
        pltpu.make_async_copy(like, like, sem).wait()

    def most(one_here, like, count, sem):
        for fewer in range(2):

            @pl.when(one_here if fewer else jnp.logical_not(one_here))
            def _():
                all_in(like.at[pl.ds(0, count - fewer)], sem)

    loads = [
        pltpu.make_async_copy(src, dst, l_sem.at[i])
        for i, (src, dst) in enumerate((
            (factor_hbm, factor_ref), (a_hbm, a_ref), (pattern_hbm, pattern_ref),
            (inv_hbm.at[child], inv_own), (inv_hbm.at[row], inv_sq),
        ))
    ]
    for c in loads:
        c.start()

    barrier = pltpu.get_barrier_semaphore()

    def greet(to):
        pl.semaphore_signal(barrier, inc=1, device_id=to, device_id_type=MESH)

    for k in range(1, 8):
        greet(device(lax.rem(x + k // 2, NX), y, z, lax.rem(h + k % 2, 2)))
    for k in (1, NZ - 1):
        greet(device(x, y, lax.rem(z + k, NZ), h))
    for k in range(1, NY):
        greet(device(x, lax.rem(y + k, NY), z, h))
    loads[0].wait()
    pl.semaphore_wait(barrier, 12)

    for k in range(1, 8):
        tx, th = lax.rem(x + k // 2, NX), lax.rem(h + k % 2, 2)
        send(factor_ref.at[2 * tx + th], fbuf.at[h, x], f_ss, f_rs, device(tx, y, z, th)).start()
    fbuf[h, x] = factor_ref[child]

    for c in loads[2:4]:
        c.wait()
    all_in(factor_ref.at[pl.ds(0, 7)], f_rs)
    pieces = []
    for hh in range(2):
        keep = pattern_ref[child, 4 * (2 * y + hh) + z_lo // 2]
        pieces.append((fbuf[hh].reshape(64, 512).astype(F32) * keep.astype(F32)).astype(BF16))
    masked = jnp.concatenate(pieces, axis=0)
    panel = jnp.dot(masked, inv_own[...], preferred_element_type=F32).astype(BF16).reshape(2, 4, 16, 512)
    for hh in range(2):
        for xx in range(4):
            pn[hh, z_lo, xx, z_hi] = panel[hh, xx]

    holds = y == z_lo // 2

    def share(zz, hh):
        @pl.when(both(holds, lax.rem(z_lo, 2) == hh, lax.rem(zz, 2) == z_hi))
        def _():
            zl, zh = lax.rem(zz, ZLO), zz // ZLO
            for k in (1, 3, 2):
                send(
                    pn.at[hh, zl, :, zh], pc.at[zl // 2, :, zh], p_ss, p_rs,
                    device(x, lax.rem(y + k, NY), z, h),
                ).start()
            pc[zl // 2, :, zh] = pn[hh, zl, :, zh]

    def shard(zz, s):
        return pn.at[s // 2, lax.rem(zz, ZLO), pl.ds(s % 2 * 2, 2), zz // ZLO]

    ring = {}
    for t in range(1, 9):
        for s in range(4):
            for d in range(2):
                src = lax.rem(z + (NZ - (t - 1) if d == 0 else t - 1), NZ)
                to = lax.rem(z + (1 if d == 0 else NZ - 1), NZ)
                if t > 1:
                    ring[d, t - 1, s].wait_recv()
                if t < 8 or d == s // 2:
                    ring[d, t, s] = send(
                        shard(src, s), shard(src, s), r_ss.at[(t - 1) // 4 + t // 8], r_rs.at[d, t - 1, s],
                        device(x, y, to, h),
                    )
                    ring[d, t, s].start()
                if s % 2 == 1 and (t > 1 or d == 0):
                    share(src, s // 2)
        if t == 1:
            loads[1].wait()
            at[h, x] = a_ref[...].T
            for k in (1, 3, 2):
                send(at.at[h, x], at.at[h, x], a_ss, a_rs, device(lax.rem(x + k, NX), y, z, h)).start()
            loads[4].wait()
            lanes = pl.multiple_of((band * 8) // 128 * 128, 128)
            square[...] = contract_rows(inv_sq[:, pl.ds(lanes, 128)], inv_sq[...])
        if t == 7:
            all_in(at.at[0, pl.ds(0, 3)], a_rs)
            for k in range(NX):
                send(at.at[h, k], at.at[h, k], c_ss, c_rs, device(x, y, z, 1 - h)).start()
    for s in range(4):
        ring[s // 2, 8, s].wait_recv()
        if s % 2 == 1:
            share(lax.rem(z + 8, NZ), s // 2)

    all_in(at.at[0], c_rs)
    for xx in range(NX):
        block = jnp.dot(at[0, xx], pn[0].reshape(1024, 512), preferred_element_type=F32)
        block += jnp.dot(at[1, xx], pn[1].reshape(1024, 512), preferred_element_type=F32)
        for yy in range(NY):
            columns = block[:, yy * 128 : yy * 128 + 128]
            part[yy, xx] = columns
            y_send[yy, xx] = columns.astype(BF16)
    for k in range(1, NY):
        ty = lax.rem(y + k, NY)
        send(y_send.at[ty], y_recv.at[k], y_ss, y_rs.at[k - 1], device(x, ty, z, h)).start()
    total = part[y]
    for k in range(1, NY):
        all_in(y_recv.at[k], y_rs.at[k - 1])
        total += y_recv[k].astype(F32)

    o_send[...] = total
    for xx in range(NX):
        here = both(xx == x, x == y)

        @pl.when(jnp.logical_not(here))
        def _():
            send(o_send.at[xx], o_recv.at[y], o_ss, o_rs, device(xx, x, z, h)).start()

        @pl.when(here)
        def _():
            o_recv[y] = o_send[xx]

    @pl.when(jnp.logical_not(holds))
    def _():
        all_in(pc, p_rs)

    cross = contract_rows(total.astype(BF16).reshape(512, 128), pc[...].reshape(512, 512)).reshape(16, 8, 512)
    for i in range(16):
        z_send[i] = jnp.concatenate([cross[i][:, :256], cross[i][:, 256:]], axis=0).astype(BF16)

    def piece(i):
        tx, tz = lax.rem(i // 2, 4), lax.rem(i, 2) * ZLO + 2 * y + i // 8
        return device(tx, x, tz, h), both(tx == x, x == y, tz == z)

    for n in range(16):
        i = lax.rem(z + n, 16)
        to, here = piece(i)

        @pl.when(jnp.logical_not(here))
        def _():
            send(z_send.at[i], z_recv.at[z], z_ss, z_rs, to).start()

        @pl.when(here)
        def _():
            z_recv[z] = z_send[i]

    keep = -pattern_ref[row, col].astype(F32)
    most(x == y, o_recv, NX, o_rs)
    for yy in range(NY):
        out_ref[0, :, yy * 128 : yy * 128 + 128] = o_recv[yy] * keep
    out_copy = pltpu.make_async_copy(out_ref, out_hbm, l_sem.at[0])
    out_copy.start()
    most(both(x == y, holds), z_recv, NZ, z_rs)
    acc = z_recv[0].astype(F32)
    for zz in range(1, NZ):
        acc += z_recv[zz].astype(F32)
    own = square[pl.ds(pl.multiple_of(lax.rem(band * 8, 128), 8), 8), :]
    diag_ref[0, :, :256] = acc[:8] + own[:, :256]
    diag_ref[0, :, 256:] = acc[8:] + own[:, 256:]

    diag_copy = pltpu.make_async_copy(diag_ref, diag_hbm, l_sem.at[1])
    diag_copy.start()
    out_copy.wait()

    all_in(factor_ref.at[pl.ds(0, 7)], f_ss)
    all_in(at.at[0, pl.ds(0, 3)], a_ss)
    all_in(at.at[0], c_ss)
    all_in(pn.at[0], r_ss.at[0])
    all_in(pn.at[:, pl.ds(0, 6), :, 0], r_ss.at[1])
    all_in(pn.at[0, 0], r_ss.at[2])
    all_in(y_send.at[pl.ds(0, 3)], y_ss)
    most(x == y, o_send, NX, o_ss)

    @pl.when(holds)
    def _():
        all_in(pn.at[:, pl.ds(0, 6)], p_ss)

    most(both(x == y, holds), z_send, NZ, z_ss)
    diag_copy.wait()


def deliver(panel_ref, diag_ref, panel_out, diag_out):
    panel_out[...] = panel_ref[...]
    diag_out[...] = diag_ref[...]


def body(ancestor, factor, inv_diag, pattern):
    vmem, dma = pltpu.VMEM, pltpu.SemaphoreType.DMA
    results = pl.pallas_call(
        kernel,
        out_shape=(
            jax.ShapeDtypeStruct((1, 128, 512), F32),
            jax.ShapeDtypeStruct((1, 8, 512), F32),
        ),
        in_specs=[pl.BlockSpec(memory_space=pl.ANY)] * 4,
        out_specs=(pl.BlockSpec(memory_space=pl.ANY), pl.BlockSpec(memory_space=pl.ANY)),
        scratch_shapes=[
            vmem((1, 128, 512), F32),
            vmem((1, 8, 512), F32),
            vmem((1024, 128), BF16),
            vmem((8, 16, 512), BF16),
            pltpu.SMEM((8, 32), jnp.int32),
            vmem((2, 4, 128, 1024), BF16),
            vmem((2, 4, 16, 512), BF16),
            vmem((2, 8, 4, 2, 16, 512), BF16),
            vmem((4, 4, 2, 16, 512), BF16),
            vmem((512, 512), BF16),
            vmem((512, 512), BF16),
            vmem((128, 512), F32),
            vmem((4, 4, 128, 128), F32),
            vmem((4, 4, 128, 128), BF16),
            vmem((4, 4, 128, 128), BF16),
            vmem((4, 128, 128), F32),
            vmem((4, 128, 128), F32),
            vmem((16, 16, 256), BF16),
            vmem((16, 16, 256), BF16),
            dma, dma,
            dma, dma,
            dma, dma,
            dma((3,)), dma((2, 8, 4)),
            dma, dma,
            dma, dma((3,)),
            dma, dma,
            dma, dma,
            dma((5,)),
        ],
        compiler_params=pltpu.CompilerParams(
            collective_id=0, has_side_effects=True, vmem_limit_bytes=60 * 1024 * 1024
        ),
        name="takahashi",
    )(ancestor, factor, inv_diag, pattern)
    return pl.pallas_call(
        deliver,
        out_shape=tuple(jax.ShapeDtypeStruct(r.shape, F32) for r in results),
        in_specs=[pl.BlockSpec(memory_space=pltpu.VMEM)] * 2,
        out_specs=(pl.BlockSpec(memory_space=pltpu.VMEM), pl.BlockSpec(memory_space=pltpu.VMEM)),
        compiler_params=pltpu.CompilerParams(vmem_limit_bytes=60 * 1024 * 1024),
        name="deliver",
    )(*results)


def solution(mesh):
    return jax.shard_map(
        body,
        mesh=mesh,
        in_specs=(P("row", ("col", "leaf")), P(None, ("row", "col", "leaf"), None), P(), P()),
        out_specs=(P("row", ("col", "leaf"), None), P("row", ("col", "leaf"), None)),
        check_vma=False,
    )
```

```python
import functools

import jax
import jax.numpy as jnp
from jax import lax
from jax.experimental import pallas as pl
from jax.experimental.pallas import tpu as pltpu
from jax.sharding import PartitionSpec as P

MESH = pl.DeviceIdType.MESH
NX, NY, NZ, ZLO = 4, 4, 16, 8
F32, BF16 = jnp.float32, jnp.bfloat16


def device(x, y, z, h):
    return (2 * y + h, 4 * lax.rem(z, ZLO) + x, z // ZLO)


def contract_rows(a, b):
    return lax.dot_general(a, b, (((0,), (0,)), ((), ())), preferred_element_type=F32)


def both(*conditions):
    return functools.reduce(jnp.logical_and, conditions)


def kernel(
    a_hbm, factor_hbm, inv_hbm, pattern_hbm, out_hbm, diag_hbm,
    out_ref, diag_ref,    a_ref, factor_ref, pattern_ref, at, fbuf, pn, pc, inv_own, inv_sq, square, part, y_send, y_recv, rounded,
    o_send, o_recv, z_send, z_recv,
    f_ss, f_rs, a_ss, a_rs, c_ss, c_rs, r_ss, r_rs, p_ss, p_rs, y_ss, y_rs, o_ss, o_rs, z_ss, z_rs, l_sem,
):
    row, col, z_hi = lax.axis_index("row"), lax.axis_index("col"), lax.axis_index("leaf")
    y, h = row // 2, lax.rem(row, 2)
    z_lo, x = col // 4, lax.rem(col, 4)
    z = z_hi * ZLO + z_lo
    band = col * 2 + z_hi
    child = 2 * x + h

    def send(src, dst, ss, rs, to):
        return pltpu.make_async_remote_copy(
            src_ref=src, dst_ref=dst, send_sem=ss, recv_sem=rs, device_id=to, device_id_type=MESH
        )

    def all_in(like, sem):
        pltpu.make_async_copy(like, like, sem).wait()

    def most(one_here, like, count, sem):
        for fewer in range(2):

            @pl.when(one_here if fewer else jnp.logical_not(one_here))
            def _():
                all_in(like.at[pl.ds(0, count - fewer)], sem)

    loads = [
        pltpu.make_async_copy(src, dst, l_sem.at[i])
        for i, (src, dst) in enumerate((
            (factor_hbm, factor_ref), (a_hbm, a_ref), (pattern_hbm, pattern_ref),
            (inv_hbm.at[child], inv_own), (inv_hbm.at[row], inv_sq),
        ))
    ]
    for c in loads:
        c.start()

    barrier = pltpu.get_barrier_semaphore()

    def greet(to):
        pl.semaphore_signal(barrier, inc=1, device_id=to, device_id_type=MESH)

    for k in range(1, 8):
        greet(device(lax.rem(x + k // 2, NX), y, z, lax.rem(h + k % 2, 2)))
    for k in (1, NZ - 1):
        greet(device(x, y, lax.rem(z + k, NZ), h))
    for k in range(1, NY):
        greet(device(x, lax.rem(y + k, NY), z, h))
    loads[0].wait()
    pl.semaphore_wait(barrier, 12)

    for k in range(1, 8):
        tx, th = lax.rem(x + k // 2, NX), lax.rem(h + k % 2, 2)
        send(factor_ref.at[2 * tx + th], fbuf.at[h, x], f_ss, f_rs, device(tx, y, z, th)).start()
    fbuf[h, x] = factor_ref[child]

    for c in loads[2:4]:
        c.wait()
    all_in(factor_ref.at[pl.ds(0, 7)], f_rs)
    pieces = []
    for hh in range(2):
        keep = pattern_ref[child, 4 * (2 * y + hh) + z_lo // 2]
        pieces.append((fbuf[hh].reshape(64, 512).astype(F32) * keep.astype(F32)).astype(BF16))
    masked = jnp.concatenate(pieces, axis=0)
    panel = jnp.dot(masked, inv_own[...], preferred_element_type=F32).astype(BF16).reshape(2, 4, 16, 512)
    for hh in range(2):
        for xx in range(4):
            pn[hh, z_lo, xx, z_hi] = panel[hh, xx]

    holds = y == z_lo // 2

    def share(zz, hh):
        @pl.when(both(holds, lax.rem(z_lo, 2) == hh, lax.rem(zz, 2) == z_hi))
        def _():
            zl, zh = lax.rem(zz, ZLO), zz // ZLO
            for k in (1, 3, 2):
                send(
                    pn.at[hh, zl, :, zh], pc.at[zl // 2, :, zh], p_ss, p_rs,
                    device(x, lax.rem(y + k, NY), z, h),
                ).start()
            pc[zl // 2, :, zh] = pn[hh, zl, :, zh]

    def shard(zz, s):
        return pn.at[s // 2, lax.rem(zz, ZLO), pl.ds(s % 2 * 2, 2), zz // ZLO]

    ring = {}
    for t in range(1, 9):
        for s in range(4):
            for d in range(2):
                src = lax.rem(z + (NZ - (t - 1) if d == 0 else t - 1), NZ)
                to = lax.rem(z + (1 if d == 0 else NZ - 1), NZ)
                if t > 1:
                    ring[d, t - 1, s].wait_recv()
                if t < 8 or d == s // 2:
                    ring[d, t, s] = send(
                        shard(src, s), shard(src, s), r_ss.at[(t - 1) // 4 + t // 8], r_rs.at[d, t - 1, s],
                        device(x, y, to, h),
                    )
                    ring[d, t, s].start()
                if s % 2 == 1 and (t > 1 or d == 0):
                    share(src, s // 2)
        if t == 1:
            loads[1].wait()
            at[h, x] = a_ref[...].T
            for k in (1, 3, 2):
                send(at.at[h, x], at.at[h, x], a_ss, a_rs, device(lax.rem(x + k, NX), y, z, h)).start()
            loads[4].wait()
            lanes = pl.multiple_of((band * 8) // 128 * 128, 128)
            square[...] = contract_rows(inv_sq[:, pl.ds(lanes, 128)], inv_sq[...])
        if t == 7:
            all_in(at.at[0, pl.ds(0, 3)], a_rs)
            for k in range(NX):
                send(at.at[h, k], at.at[h, k], c_ss, c_rs, device(x, y, z, 1 - h)).start()
    for s in range(4):
        ring[s // 2, 8, s].wait_recv()
        if s % 2 == 1:
            share(lax.rem(z + 8, NZ), s // 2)

    all_in(at.at[0], c_rs)
    for xx in range(NX):
        block = jnp.dot(at[0, xx], pn[0].reshape(1024, 512), preferred_element_type=F32)
        block += jnp.dot(at[1, xx], pn[1].reshape(1024, 512), preferred_element_type=F32)
        for yy in range(NY):
            columns = block[:, yy * 128 : yy * 128 + 128]
            part[yy, xx] = columns
            y_send[yy, xx] = columns.astype(BF16)
        if xx % 2 == 1:
            for k in range(1, NY):
                ty, half = lax.rem(y + k, NY), pl.ds(xx - 1, 2)
                send(
                    y_send.at[ty, half], y_recv.at[k, half], y_ss, y_rs.at[k - 1, xx // 2], device(x, ty, z, h)
                ).start()
    for half in range(2):
        pair = pl.ds(2 * half, 2)
        total = part[y, pair]
        for k in range(1, NY):
            all_in(y_recv.at[k, pair], y_rs.at[k - 1, half])
            total += y_recv[k, pair].astype(F32)
        o_send[pair] = total.astype(o_send.dtype)
        rounded[pair] = total.astype(BF16)

    for xx in range(NX):
        here = both(xx == x, x == y)

        @pl.when(jnp.logical_not(here))
        def _():
            send(o_send.at[xx], o_recv.at[y], o_ss, o_rs, device(xx, x, z, h)).start()

        @pl.when(here)
        def _():
            o_recv[y] = o_send[xx]

    @pl.when(jnp.logical_not(holds))
    def _():
        all_in(pc, p_rs)

    cross = contract_rows(rounded[...].reshape(512, 128), pc[...].reshape(512, 512)).reshape(16, 8, 512)
    for i in range(16):
        z_send[i] = jnp.concatenate([cross[i][:, :256], cross[i][:, 256:]], axis=0).astype(BF16)

    def piece(i):
        tx, tz = lax.rem(i // 2, 4), lax.rem(i, 2) * ZLO + 2 * y + i // 8
        return device(tx, x, tz, h), both(tx == x, x == y, tz == z)

    for n in range(16):
        i = lax.rem(z + n, 16)
        to, here = piece(i)

        @pl.when(jnp.logical_not(here))
        def _():
            send(z_send.at[i], z_recv.at[z], z_ss, z_rs, to).start()

        @pl.when(here)
        def _():
            z_recv[z] = z_send[i]

    keep = -pattern_ref[row, col].astype(F32)
    most(x == y, o_recv, NX, o_rs)
    for yy in range(NY):
        out_ref[0, :, yy * 128 : yy * 128 + 128] = o_recv[yy].astype(F32) * keep
    out_copy = pltpu.make_async_copy(out_ref, out_hbm, l_sem.at[0])
    out_copy.start()
    most(both(x == y, holds), z_recv, NZ, z_rs)
    acc = z_recv[0].astype(F32)
    for zz in range(1, NZ):
        acc += z_recv[zz].astype(F32)
    own = square[pl.ds(pl.multiple_of(lax.rem(band * 8, 128), 8), 8), :]
    diag_ref[0, :, :256] = acc[:8] + own[:, :256]
    diag_ref[0, :, 256:] = acc[8:] + own[:, 256:]

    diag_copy = pltpu.make_async_copy(diag_ref, diag_hbm, l_sem.at[1])
    diag_copy.start()
    out_copy.wait()

    all_in(factor_ref.at[pl.ds(0, 7)], f_ss)
    all_in(at.at[0, pl.ds(0, 3)], a_ss)
    all_in(at.at[0], c_ss)
    all_in(pn.at[0], r_ss.at[0])
    all_in(pn.at[:, pl.ds(0, 6), :, 0], r_ss.at[1])
    all_in(pn.at[0, 0], r_ss.at[2])
    all_in(y_send.at[pl.ds(0, 3)], y_ss)
    most(x == y, o_send, NX, o_ss)

    @pl.when(holds)
    def _():
        all_in(pn.at[:, pl.ds(0, 6)], p_ss)

    most(both(x == y, holds), z_send, NZ, z_ss)
    diag_copy.wait()


def deliver(panel_ref, diag_ref, panel_out, diag_out):
    panel_out[...] = panel_ref[...]
    diag_out[...] = diag_ref[...]


def body(ancestor, factor, inv_diag, pattern):
    vmem, dma = pltpu.VMEM, pltpu.SemaphoreType.DMA
    results = pl.pallas_call(
        kernel,
        out_shape=(
            jax.ShapeDtypeStruct((1, 128, 512), F32),
            jax.ShapeDtypeStruct((1, 8, 512), F32),
        ),
        in_specs=[pl.BlockSpec(memory_space=pl.ANY)] * 4,
        out_specs=(pl.BlockSpec(memory_space=pl.ANY), pl.BlockSpec(memory_space=pl.ANY)),
        scratch_shapes=[
            vmem((1, 128, 512), F32),
            vmem((1, 8, 512), F32),
            vmem((1024, 128), BF16),
            vmem((8, 16, 512), BF16),
            pltpu.SMEM((8, 32), jnp.int32),
            vmem((2, 4, 128, 1024), BF16),
            vmem((2, 4, 16, 512), BF16),
            vmem((2, 8, 4, 2, 16, 512), BF16),
            vmem((4, 4, 2, 16, 512), BF16),
            vmem((512, 512), BF16),
            vmem((512, 512), BF16),
            vmem((128, 512), F32),
            vmem((4, 4, 128, 128), F32),
            vmem((4, 4, 128, 128), BF16),
            vmem((4, 4, 128, 128), BF16),
            vmem((4, 128, 128), BF16),
            vmem((4, 128, 128), BF16),
            vmem((4, 128, 128), BF16),
            vmem((16, 16, 256), BF16),
            vmem((16, 16, 256), BF16),
            dma, dma,
            dma, dma,
            dma, dma,
            dma((3,)), dma((2, 8, 4)),
            dma, dma,
            dma, dma((3, 2)),
            dma, dma,
            dma, dma,
            dma((5,)),
        ],
        compiler_params=pltpu.CompilerParams(
            collective_id=0, has_side_effects=True, vmem_limit_bytes=60 * 1024 * 1024
        ),
        name="takahashi",
    )(ancestor, factor, inv_diag, pattern)
    return pl.pallas_call(
        deliver,
        out_shape=tuple(jax.ShapeDtypeStruct(r.shape, F32) for r in results),
        in_specs=[pl.BlockSpec(memory_space=pltpu.VMEM)] * 2,
        out_specs=(pl.BlockSpec(memory_space=pltpu.VMEM), pl.BlockSpec(memory_space=pltpu.VMEM)),
        compiler_params=pltpu.CompilerParams(vmem_limit_bytes=60 * 1024 * 1024),
        name="deliver",
    )(*results)


def solution(mesh):
    return jax.shard_map(
        body,
        mesh=mesh,
        in_specs=(P("row", ("col", "leaf")), P(None, ("row", "col", "leaf"), None), P(), P()),
        out_specs=(P("row", ("col", "leaf"), None), P("row", ("col", "leaf"), None)),
        check_vma=False,
    )
```

```python
import functools

import jax
import jax.numpy as jnp
from jax import lax
from jax.experimental import pallas as pl
from jax.experimental.pallas import tpu as pltpu
from jax.sharding import PartitionSpec as P

MESH = pl.DeviceIdType.MESH
NX, NY, NZ, ZLO = 4, 4, 16, 8
F32, BF16 = jnp.float32, jnp.bfloat16


def device(x, y, z, h):
    return (2 * y + h, 4 * lax.rem(z, ZLO) + x, z // ZLO)


def contract_rows(a, b):
    return lax.dot_general(a, b, (((0,), (0,)), ((), ())), preferred_element_type=F32)


def both(*conditions):
    return functools.reduce(jnp.logical_and, conditions)


def kernel(
    a_hbm, factor_hbm, inv_hbm, pattern_hbm, out_hbm, diag_hbm,
    out_ref, diag_ref,    a_ref, factor_ref, pattern_ref, at, fbuf, pn, pc, inv_own, inv_sq, square, part, y_send, y_recv, rounded,
    o_send, o_recv, z_send, z_recv,
    f_ss, f_rs, a_ss, a_rs, c_ss, c_rs, r_ss, r_rs, p_ss, p_rs, y_ss, y_rs, o_ss, o_rs, z_ss, z_rs, l_sem,
):
    row, col, z_hi = lax.axis_index("row"), lax.axis_index("col"), lax.axis_index("leaf")
    y, h = row // 2, lax.rem(row, 2)
    z_lo, x = col // 4, lax.rem(col, 4)
    z = z_hi * ZLO + z_lo
    band = col * 2 + z_hi
    child = 2 * x + h

    def send(src, dst, ss, rs, to):
        return pltpu.make_async_remote_copy(
            src_ref=src, dst_ref=dst, send_sem=ss, recv_sem=rs, device_id=to, device_id_type=MESH
        )

    def all_in(like, sem):
        pltpu.make_async_copy(like, like, sem).wait()

    def most(one_here, like, count, sem):
        for fewer in range(2):

            @pl.when(one_here if fewer else jnp.logical_not(one_here))
            def _():
                all_in(like.at[pl.ds(0, count - fewer)], sem)

    loads = [
        pltpu.make_async_copy(src, dst, l_sem.at[i])
        for i, (src, dst) in enumerate((
            (factor_hbm, factor_ref), (a_hbm, a_ref), (pattern_hbm, pattern_ref),
            (inv_hbm.at[child], inv_own), (inv_hbm.at[row], inv_sq),
        ))
    ]
    for c in loads:
        c.start()

    barrier = pltpu.get_barrier_semaphore()

    def greet(to):
        pl.semaphore_signal(barrier, inc=1, device_id=to, device_id_type=MESH)

    for k in range(1, 8):
        greet(device(lax.rem(x + k // 2, NX), y, z, lax.rem(h + k % 2, 2)))
    for k in (1, NZ - 1):
        greet(device(x, y, lax.rem(z + k, NZ), h))
    for k in range(1, NY):
        greet(device(x, lax.rem(y + k, NY), z, h))
    loads[0].wait()
    pl.semaphore_wait(barrier, 12)

    for k in range(1, 8):
        tx, th = lax.rem(x + k // 2, NX), lax.rem(h + k % 2, 2)
        send(factor_ref.at[2 * tx + th], fbuf.at[h, x], f_ss, f_rs, device(tx, y, z, th)).start()
    fbuf[h, x] = factor_ref[child]

    for c in loads[2:4]:
        c.wait()
    all_in(factor_ref.at[pl.ds(0, 7)], f_rs)
    pieces = []
    for hh in range(2):
        keep = pattern_ref[child, 4 * (2 * y + hh) + z_lo // 2]
        pieces.append((fbuf[hh].reshape(64, 512).astype(F32) * keep.astype(F32)).astype(BF16))
    masked = jnp.concatenate(pieces, axis=0)
    panel = jnp.dot(masked, inv_own[...], preferred_element_type=F32).astype(BF16).reshape(2, 4, 16, 512)
    for hh in range(2):
        for xx in range(4):
            pn[hh, z_lo, xx, z_hi] = panel[hh, xx]

    holds = y == z_lo // 2

    def share(zz, hh):
        @pl.when(both(holds, lax.rem(z_lo, 2) == hh, lax.rem(zz, 2) == z_hi))
        def _():
            zl, zh = lax.rem(zz, ZLO), zz // ZLO
            for k in (1, 3, 2):
                send(
                    pn.at[hh, zl, :, zh], pc.at[zl // 2, :, zh], p_ss, p_rs,
                    device(x, lax.rem(y + k, NY), z, h),
                ).start()
            pc[zl // 2, :, zh] = pn[hh, zl, :, zh]

    def shard(zz, s):
        return pn.at[s // 2, lax.rem(zz, ZLO), pl.ds(s % 2 * 2, 2), zz // ZLO]

    ring = {}
    for t in range(1, 9):
        for s in range(4):
            for d in range(2):
                src = lax.rem(z + (NZ - (t - 1) if d == 0 else t - 1), NZ)
                to = lax.rem(z + (1 if d == 0 else NZ - 1), NZ)
                if t > 1:
                    ring[d, t - 1, s].wait_recv()
                if t < 8 or d == s // 2:
                    ring[d, t, s] = send(
                        shard(src, s), shard(src, s), r_ss.at[(t - 1) // 4 + t // 8], r_rs.at[d, t - 1, s],
                        device(x, y, to, h),
                    )
                    ring[d, t, s].start()
                if s % 2 == 1 and (t > 1 or d == 0):
                    share(src, s // 2)
        if t == 1:
            loads[1].wait()
            at[h, x] = a_ref[...].T
            for k in (1, 3, 2):
                send(at.at[h, x], at.at[h, x], a_ss, a_rs, device(lax.rem(x + k, NX), y, z, h)).start()
            loads[4].wait()
            lanes = pl.multiple_of((band * 8) // 128 * 128, 128)
            square[...] = contract_rows(inv_sq[:, pl.ds(lanes, 128)], inv_sq[...])
        if t == 7:
            all_in(at.at[0, pl.ds(0, 3)], a_rs)
            for k in range(NX):
                send(at.at[h, k], at.at[h, k], c_ss, c_rs, device(x, y, z, 1 - h)).start()
    for s in range(4):
        ring[s // 2, 8, s].wait_recv()
        if s % 2 == 1:
            share(lax.rem(z + 8, NZ), s // 2)

    all_in(at.at[0], c_rs)
    for xx in range(NX):
        block = jnp.dot(at[0, xx], pn[0].reshape(1024, 512), preferred_element_type=F32)
        block += jnp.dot(at[1, xx], pn[1].reshape(1024, 512), preferred_element_type=F32)
        for yy in range(NY):
            columns = block[:, yy * 128 : yy * 128 + 128]
            part[yy, xx] = columns
            y_send[yy, xx] = columns.astype(BF16)
        if xx % 2 == 1:
            for k in (2, 1, 3):
                ty, half = lax.rem(y + k, NY), pl.ds(xx - 1, 2)
                send(
                    y_send.at[ty, half], y_recv.at[k, half], y_ss, y_rs.at[k - 1, xx // 2], device(x, ty, z, h)
                ).start()
    for half in range(2):
        pair = pl.ds(2 * half, 2)
        total = part[y, pair]
        for k in (1, 3, 2):
            all_in(y_recv.at[k, pair], y_rs.at[k - 1, half])
            total += y_recv[k, pair].astype(F32)
        o_send[pair] = total.astype(o_send.dtype)
        rounded[pair] = total.astype(BF16)

    for xx in range(NX):
        here = both(xx == x, x == y)

        @pl.when(jnp.logical_not(here))
        def _():
            send(o_send.at[xx], o_recv.at[y], o_ss, o_rs, device(xx, x, z, h)).start()

        @pl.when(here)
        def _():
            o_recv[y] = o_send[xx]

    @pl.when(jnp.logical_not(holds))
    def _():
        all_in(pc, p_rs)

    cross = contract_rows(rounded[...].reshape(512, 128), pc[...].reshape(512, 512)).reshape(16, 8, 512)
    for i in range(16):
        z_send[i] = jnp.concatenate([cross[i][:, :256], cross[i][:, 256:]], axis=0).astype(BF16)

    def piece(i):
        tx, tz = lax.rem(i // 2, 4), lax.rem(i, 2) * ZLO + 2 * y + i // 8
        return device(tx, x, tz, h), both(tx == x, x == y, tz == z)

    for n in range(16):
        i = lax.rem(z + n, 16)
        to, here = piece(i)

        @pl.when(jnp.logical_not(here))
        def _():
            send(z_send.at[i], z_recv.at[z], z_ss, z_rs, to).start()

        @pl.when(here)
        def _():
            z_recv[z] = z_send[i]

    keep = -pattern_ref[row, col].astype(F32)
    most(x == y, o_recv, NX, o_rs)
    for yy in range(NY):
        out_ref[0, :, yy * 128 : yy * 128 + 128] = o_recv[yy].astype(F32) * keep
    out_copy = pltpu.make_async_copy(out_ref, out_hbm, l_sem.at[0])
    out_copy.start()
    most(both(x == y, holds), z_recv, NZ, z_rs)
    acc = z_recv[0].astype(F32)
    for zz in range(1, NZ):
        acc += z_recv[zz].astype(F32)
    own = square[pl.ds(pl.multiple_of(lax.rem(band * 8, 128), 8), 8), :]
    diag_ref[0, :, :256] = acc[:8] + own[:, :256]
    diag_ref[0, :, 256:] = acc[8:] + own[:, 256:]

    diag_copy = pltpu.make_async_copy(diag_ref, diag_hbm, l_sem.at[1])
    diag_copy.start()
    out_copy.wait()

    all_in(factor_ref.at[pl.ds(0, 7)], f_ss)
    all_in(at.at[0, pl.ds(0, 3)], a_ss)
    all_in(at.at[0], c_ss)
    all_in(pn.at[0], r_ss.at[0])
    all_in(pn.at[:, pl.ds(0, 6), :, 0], r_ss.at[1])
    all_in(pn.at[0, 0], r_ss.at[2])
    all_in(y_send.at[pl.ds(0, 3)], y_ss)
    most(x == y, o_send, NX, o_ss)

    @pl.when(holds)
    def _():
        all_in(pn.at[:, pl.ds(0, 6)], p_ss)

    most(both(x == y, holds), z_send, NZ, z_ss)
    diag_copy.wait()


def deliver(panel_ref, diag_ref, panel_out, diag_out):
    panel_out[...] = panel_ref[...]
    diag_out[...] = diag_ref[...]


def body(ancestor, factor, inv_diag, pattern):
    vmem, dma = pltpu.VMEM, pltpu.SemaphoreType.DMA
    results = pl.pallas_call(
        kernel,
        out_shape=(
            jax.ShapeDtypeStruct((1, 128, 512), F32),
            jax.ShapeDtypeStruct((1, 8, 512), F32),
        ),
        in_specs=[pl.BlockSpec(memory_space=pl.ANY)] * 4,
        out_specs=(pl.BlockSpec(memory_space=pl.ANY), pl.BlockSpec(memory_space=pl.ANY)),
        scratch_shapes=[
            vmem((1, 128, 512), F32),
            vmem((1, 8, 512), F32),
            vmem((1024, 128), BF16),
            vmem((8, 16, 512), BF16),
            pltpu.SMEM((8, 32), jnp.int32),
            vmem((2, 4, 128, 1024), BF16),
            vmem((2, 4, 16, 512), BF16),
            vmem((2, 8, 4, 2, 16, 512), BF16),
            vmem((4, 4, 2, 16, 512), BF16),
            vmem((512, 512), BF16),
            vmem((512, 512), BF16),
            vmem((128, 512), F32),
            vmem((4, 4, 128, 128), F32),
            vmem((4, 4, 128, 128), BF16),
            vmem((4, 4, 128, 128), BF16),
            vmem((4, 128, 128), BF16),
            vmem((4, 128, 128), BF16),
            vmem((4, 128, 128), BF16),
            vmem((16, 16, 256), BF16),
            vmem((16, 16, 256), BF16),
            dma, dma,
            dma, dma,
            dma, dma,
            dma((3,)), dma((2, 8, 4)),
            dma, dma,
            dma, dma((3, 2)),
            dma, dma,
            dma, dma,
            dma((5,)),
        ],
        compiler_params=pltpu.CompilerParams(
            collective_id=0, has_side_effects=True, vmem_limit_bytes=60 * 1024 * 1024
        ),
        name="takahashi",
    )(ancestor, factor, inv_diag, pattern)
    return pl.pallas_call(
        deliver,
        out_shape=tuple(jax.ShapeDtypeStruct(r.shape, F32) for r in results),
        in_specs=[pl.BlockSpec(memory_space=pltpu.VMEM)] * 2,
        out_specs=(pl.BlockSpec(memory_space=pltpu.VMEM), pl.BlockSpec(memory_space=pltpu.VMEM)),
        compiler_params=pltpu.CompilerParams(vmem_limit_bytes=60 * 1024 * 1024),
        name="deliver",
    )(*results)


def solution(mesh):
    return jax.shard_map(
        body,
        mesh=mesh,
        in_specs=(P("row", ("col", "leaf")), P(None, ("row", "col", "leaf"), None), P(), P()),
        out_specs=(P("row", ("col", "leaf"), None), P("row", ("col", "leaf"), None)),
        check_vma=False,
    )
```
